512 devices in a mesh: ax: 32 (over y, z_lo), circ: 8 (over z_hi, x), rad: 2 (over core).
Axes of the slice: x: 4, y: 4, z: 16 (z_hi: 2, z_lo: 8; z = z_hi * 8 + z_lo), core: 2. Of those that a mesh axis runs over, the one named last changes fastest.
Arguments:
- adjoint_rhs: bfloat16 [64, 48, 128, 256], P('ax', 'circ', None, 'rad'), may hold values from -6 to 6
- pivot_inverse: bfloat16 [64, 48, 256, 256], P('ax', 'circ', None, 'rad'), may hold values from -1 to 2
- diagonal_block: bfloat16 [64, 48, 256, 256], P('ax', 'circ', None, 'rad'), may hold values from -1 to 2
- coupling: bfloat16 [64, 48, 2, 4, 128, 128], P('ax', 'circ', 'rad'), may hold values from -0.21875 to 0.21875
- pattern: int32 [64, 48, 2, 4], P('ax', 'circ', 'rad'), may hold values 0 or 1
- wave_level: int32 [64, 48], P('ax', 'circ'), may hold values from 0 to 3, as said below
Outputs:
- first_vector: bfloat16 [64, 48, 128, 256], P('ax', 'circ', None, 'rad')
- second_vector: bfloat16 [64, 48, 128, 256], P('ax', 'circ', None, 'rad')
The draws below stay inside these ranges and needn't reach their ends.
Inputs may be any that keep to these rules, and one draw needn't show every extreme that they name: `wave_level`: in each aligned block of 2 x 6 tiles (the tiles of one index of ax and circ) every level holds exactly 3 tiles, and tiles that share a side, around the circumference too, have levels of different parity.
All inputs are finite; a program needn't handle non-finite values. No bound on the sum of `pattern` on one device may be relied on, other than what follows from the above.
Results may differ from the reference program's by a relative error of at most 0.017.
Values may be sent and summed in bfloat16 or wider, within the bound.
A program may use at most 64 MiB of HBM per device.

```python
import math
import jax
import jax.numpy as jnp
from jax import lax

CELLS = 128
RHS = 128
TA = 2
TC = 6
NLEV = 4
NR = 2
TILE = 256
NA = 64
NC = 48


def tile_matrix(key, offset_tag):
    base_key = jax.random.fold_in(key, offset_tag)
    key_spread = jax.random.fold_in(base_key, 1)
    key_diagonal = jax.random.fold_in(base_key, 2)
    block_shape = (NA, NC, TILE, TILE)
    spread_part = jax.random.normal(key_spread, block_shape, jnp.float32) * (0.35 / math.sqrt(TILE))
    diagonal = jax.random.uniform(key_diagonal, (NA, NC, TILE), jnp.float32, 0.7, 1.4)
    identity = (lax.broadcasted_iota(jnp.int32, (TILE, TILE), 0) == lax.broadcasted_iota(jnp.int32, (TILE, TILE), 1)).astype(jnp.float32)
    return (spread_part + identity * diagonal[..., :, None]).astype(jnp.bfloat16)


def draw_pivot_inverse(key, part):
    return tile_matrix(key, 11)


def draw_diagonal_block(key, part):
    return tile_matrix(key, 23)


def parity_slots(parity_value):
    half_row = TC // 2
    count = TA * TC // 2
    position = jnp.arange(count, dtype=jnp.int32)
    row_index = position // half_row
    column = 2 * (position % half_row) + (row_index + parity_value) % 2
    return (row_index * TC + column).astype(jnp.int32)


def draw_wave_level(key, part):
    blocks_axial = NA // TA
    blocks_circ = NC // TC
    tile_count = TA * TC
    half_count = tile_count // 2
    per_level = tile_count // NLEV
    even_slots = parity_slots(0)
    odd_slots = parity_slots(1)

    def block_levels(index):
        rank_even = jax.random.permutation(jax.random.fold_in(key, 2 * index), half_count)
        rank_odd = jax.random.permutation(jax.random.fold_in(key, 2 * index + 1), half_count)
        levels = jnp.zeros((tile_count,), jnp.int32)
        levels = levels.at[even_slots].set((2 * (rank_even // per_level)).astype(jnp.int32))
        levels = levels.at[odd_slots].set((2 * (rank_odd // per_level) + 1).astype(jnp.int32))
        return levels
    blocks = jax.vmap(block_levels)(jnp.arange(blocks_axial * blocks_circ, dtype=jnp.int32))
    blocks = blocks.reshape(blocks_axial, blocks_circ, TA, TC)
    return jnp.transpose(blocks, (0, 2, 1, 3)).reshape(NA, NC)


def with_ends(array, rng, least, top_value):
    longest = array.shape.index(max(array.shape))
    spots = []
    for shift in (0, 1):
        where = [jax.random.randint(jax.random.fold_in(rng, axis), (), 0, length) for axis, length in enumerate(array.shape)]
        where[longest] = (where[longest] + shift) % array.shape[longest]
        spots.append(tuple(where))
    return array.at[spots[0]].set(least).at[spots[1]].set(top_value)


def shard_levels(key, extent, pieces, least, high):
    gain = 1.0
    for dim, parts in pieces:
        draws = jax.random.uniform(jax.random.fold_in(jax.random.fold_in(key, 6), dim), (parts,), jnp.float32, least / len(pieces), high / len(pieces))
        gain = gain * jnp.repeat(jnp.exp(draws), extent[dim] // parts).reshape((-1,) + (1,) * (len(extent) - 1 - dim))
    return gain


def gaussian(own_key, shape, spread, most, split=(), kind=jnp.bfloat16):
    entries = spread * jax.random.normal(own_key, shape, jnp.float32)
    if split:
        entries = entries * shard_levels(own_key, shape, split, -0.22, 0.18)
    return jnp.clip(entries, -most, most).astype(kind)


def setup_inputs(seed: int = 0) -> dict:
    key_of = jax.random.split(jax.random.key(seed), 7)
    adjoint_rhs = gaussian(key_of[0], (NA, NC, RHS, TILE), 1.0, 6.0, ((0, 32), (1, 8), (3, 2)))
    pivot_inverse = draw_pivot_inverse(jax.random.fold_in(key_of[6], 71), 0)
    diagonal_block = draw_diagonal_block(jax.random.fold_in(key_of[6], 71), 0)
    coupling = gaussian(key_of[3], (NA, NC, NR, 4, CELLS, CELLS), (6 * CELLS) ** -0.5, 0.21875, ((0, 32), (1, 8), (2, 2)))
    pattern = with_ends((jax.random.randint(key_of[4], (NA, NC, NR, 4), 0, 8) < 7).astype(jnp.int32), jax.random.fold_in(key_of[4], 1), 0, 1)
    wave_level = draw_wave_level(jax.random.fold_in(key_of[6], 71), 0)
    return dict(adjoint_rhs=adjoint_rhs, pivot_inverse=pivot_inverse, diagonal_block=diagonal_block, coupling=coupling, pattern=pattern, wave_level=wave_level)


def neighbour_rows(flat_values, chosen):
    axial = chosen // NC
    circum = chosen % NC
    lower_exists = axial > 0
    upper_exists = axial < NA - 1
    lower_axial = jnp.where(lower_exists, chosen - NC, chosen)
    upper_axial = jnp.where(upper_exists, chosen + NC, chosen)
    lower_circ = axial * NC + (circum + NC - 1) % NC
    upper_circ = axial * NC + (circum + 1) % NC
    indices = jnp.stack([lower_axial, upper_axial, lower_circ, upper_circ], axis=1).astype(jnp.int32)
    always = jnp.ones_like(lower_exists)
    existing = jnp.stack([lower_exists, upper_exists, always, always], axis=1).astype(jnp.float32)
    return flat_values[indices], existing


def coupled(flat_values, chosen, coupling_flat, pattern_flat):
    picked = chosen.shape[0]
    beside, existing = neighbour_rows(flat_values, chosen)
    beside = beside.astype(jnp.float32).reshape(picked, 4, RHS, NR, CELLS)
    present = pattern_flat[chosen].astype(jnp.float32) * existing[:, None, :]
    beside = beside * jnp.transpose(present, (0, 2, 1))[:, :, None, :, None]
    weights = coupling_flat[chosen].astype(jnp.float32)
    summed = jnp.einsum('pdkrx,prdxc->pkrc', beside, weights)
    return summed.reshape(picked, RHS, TILE)


def apply_inverse(source, chosen_list, pivots, coupling_flat, pattern_flat):
    forward = jnp.zeros(source.shape, jnp.bfloat16)
    for section_index in range(NLEV):
        chosen = chosen_list[section_index]
        carried = source[chosen].astype(jnp.float32) - coupled(forward, chosen, coupling_flat, pattern_flat)
        carried = carried.astype(jnp.bfloat16)
        updated = jnp.einsum('pkx,pxc->pkc', carried.astype(jnp.float32), pivots[chosen].astype(jnp.float32))
        forward = forward.at[chosen].set(updated.astype(jnp.bfloat16))
    backward = jnp.zeros(source.shape, jnp.bfloat16)
    for section_index in reversed(range(NLEV)):
        chosen = chosen_list[section_index]
        carried = coupled(backward, chosen, coupling_flat, pattern_flat).astype(jnp.bfloat16)
        solved = jnp.einsum('pkx,pxc->pkc', carried.astype(jnp.float32), pivots[chosen].astype(jnp.float32))
        updated = forward[chosen].astype(jnp.float32) - solved
        backward = backward.at[chosen].set(updated.astype(jnp.bfloat16))
    return backward


def reference(adjoint_rhs, pivot_inverse, diagonal_block, coupling, pattern, wave_level):
    tile_count = NA * NC
    per_level = tile_count // NLEV
    keys = wave_level.reshape(-1).astype(jnp.int32) * tile_count + jnp.arange(tile_count, dtype=jnp.int32)
    ordering = jnp.argsort(keys).astype(jnp.int32)
    chosen_list = [ordering[section_index * per_level:(section_index + 1) * per_level] for section_index in range(NLEV)]
    rhs_flat = adjoint_rhs.reshape(tile_count, RHS, TILE)
    pivots = pivot_inverse.reshape(tile_count, TILE, TILE)
    diagonals = diagonal_block.reshape(tile_count, TILE, TILE)
    coupling_flat = coupling.reshape(tile_count, NR, 4, CELLS, CELLS)
    pattern_flat = pattern.reshape(tile_count, NR, 4)
    first_vector = apply_inverse(rhs_flat, chosen_list, pivots, coupling_flat, pattern_flat)
    operator_image = jnp.zeros(rhs_flat.shape, jnp.bfloat16)
    for section_index in range(NLEV):
        chosen = chosen_list[section_index]
        own_part = jnp.einsum('pkx,pxc->pkc', first_vector[chosen].astype(jnp.float32), diagonals[chosen].astype(jnp.float32))
        total = own_part + coupled(first_vector, chosen, coupling_flat, pattern_flat)
        operator_image = operator_image.at[chosen].set(total.astype(jnp.bfloat16))
    second_vector = apply_inverse(operator_image, chosen_list, pivots, coupling_flat, pattern_flat)
    return first_vector.reshape(NA, NC, RHS, TILE), second_vector.reshape(NA, NC, RHS, TILE)
```

```python
import jax
import jax.numpy as jnp
from jax import lax
from jax.experimental import pallas as pl
from jax.experimental.pallas import tpu as pltpu
from jax.sharding import PartitionSpec as P

NLEV = 4


def with_halo(block, sides, width, periodic):
    for axis, dim in sides:
        count = lax.axis_size(axis)
        forward = [(i, i + 1) for i in range(count - 1)]
        if periodic:
            forward.append((count - 1, 0))
        backward = [(target, source) for source, target in forward]
        low = lax.ppermute(
            lax.slice_in_dim(block, block.shape[dim] - width, None, axis=dim), axis, forward
        )
        high = lax.ppermute(lax.slice_in_dim(block, 0, width, axis=dim), axis, backward)
        block = jnp.concatenate([low, block, high], axis=dim)
    return block


def per_device(adjoint_rhs, pivot_inverse, diagonal_block, coupling, pattern, wave_level):
    tiles_axial, tiles_circ, rhs_count, cell_count = adjoint_rhs.shape
    tile_count = tiles_axial * tiles_circ
    per_level = tile_count // NLEV
    keys = wave_level.reshape(-1) * tile_count + jnp.arange(tile_count, dtype=jnp.int32)
    ordering = jnp.argsort(keys)
    chosen_list = [
        ordering[section_index * per_level : (section_index + 1) * per_level]
        for section_index in range(NLEV)
    ]
    rhs_flat = adjoint_rhs.reshape(tile_count, rhs_count, cell_count)
    pivots = pivot_inverse.reshape(tile_count, pivot_inverse.shape[2], cell_count)
    diagonals = diagonal_block.reshape(tile_count, diagonal_block.shape[2], cell_count)
    weights = coupling.reshape(tile_count, 4, cell_count, cell_count)
    present = pattern.reshape(tile_count, 4).astype(jnp.bfloat16)

    def neighbours_whole(values):
        tile_grid = values.reshape(tiles_axial, tiles_circ, rhs_count, cell_count)
        axial_pad = with_halo(tile_grid, (("ax", 0),), 1, False)
        circ_pad = with_halo(tile_grid, (("circ", 1),), 1, True)
        lower_axial = axial_pad[:-2]
        upper_axial = axial_pad[2:]
        lower_circ = circ_pad[:, :-2]
        upper_circ = circ_pad[:, 2:]
        stacked = jnp.stack([lower_axial, upper_axial, lower_circ, upper_circ], axis=2)
        return stacked.reshape(tile_count, 4, rhs_count, cell_count)

    def neighbours_sweep(values):
        return neighbours_whole(values)

    def couple(beside, present_rows, weight_rows):
        masked = beside * present_rows[:, :, None, None]
        return jnp.einsum("tdkx,tdxc->tkc", masked, weight_rows, preferred_element_type=jnp.float32)

    def pivot_apply(carried, chosen):
        whole_tile = lax.all_gather(carried, "rad", axis=2, tiled=True)
        return jnp.einsum(
            "tkx,txc->tkc", whole_tile, pivots[chosen], preferred_element_type=jnp.float32
        )

    def apply_inverse(source):
        forward = jnp.zeros((tile_count, rhs_count, cell_count), jnp.bfloat16)
        for section_index in range(NLEV):
            chosen = chosen_list[section_index]
            carried = source[chosen].astype(jnp.float32)
            if section_index > 0:
                beside = neighbours_sweep(forward)[chosen]
                carried = carried - couple(beside, present[chosen], weights[chosen])
            updated = pivot_apply(carried.astype(jnp.bfloat16), chosen).astype(jnp.bfloat16)
            forward = forward.at[chosen].set(updated)
        backward = jnp.zeros((tile_count, rhs_count, cell_count), jnp.bfloat16)
        for section_index in reversed(range(NLEV)):
            chosen = chosen_list[section_index]
            updated = forward[chosen].astype(jnp.float32)
            if section_index < NLEV - 1:
                beside = neighbours_sweep(backward)[chosen]
                carried = couple(beside, present[chosen], weights[chosen]).astype(jnp.bfloat16)
                updated = updated - pivot_apply(carried, chosen)
            backward = backward.at[chosen].set(updated.astype(jnp.bfloat16))
        return backward

    first_vector = apply_inverse(rhs_flat)
    whole_first = gather_layers(first_vector)
    own_part = jnp.einsum(
        "tkx,txc->tkc", whole_first, diagonals, preferred_element_type=jnp.float32
    )
    operator_image = (own_part + couple(neighbours_whole(first_vector), present, weights)).astype(
        jnp.bfloat16
    )
    second_vector = apply_inverse(operator_image)
    out_shape = (tiles_axial, tiles_circ, rhs_count, cell_count)
    return (first_vector.reshape(out_shape), second_vector.reshape(out_shape))


def swap_kernel(x_ref, o_ref, send_sem, recv_sem):
    other = {"rad": 1 - lax.axis_index("rad")}
    barrier = pltpu.get_barrier_semaphore()
    pl.semaphore_signal(barrier, inc=1, device_id=other, device_id_type=pl.DeviceIdType.MESH)
    pl.semaphore_wait(barrier, 1)
    copy = pltpu.make_async_remote_copy(x_ref, o_ref, send_sem, recv_sem, device_id=other, device_id_type=pl.DeviceIdType.MESH)
    copy.start()
    copy.wait()


def gather_layers(x):
    other = pl.pallas_call(
        swap_kernel,
        out_shape=jax.ShapeDtypeStruct(x.shape, x.dtype),
        in_specs=[pl.BlockSpec(memory_space=pltpu.VMEM)],
        out_specs=pl.BlockSpec(memory_space=pltpu.VMEM),
        scratch_shapes=[pltpu.SemaphoreType.DMA, pltpu.SemaphoreType.DMA],
        compiler_params=pltpu.CompilerParams(collective_id=0, has_side_effects=True),
    )(x)
    first = lax.axis_index("rad") == 0
    return jnp.concatenate([jnp.where(first, x, other), jnp.where(first, other, x)], axis=2)


def solution(mesh):
    return jax.shard_map(
        per_device,
        mesh=mesh,
        in_specs=(
            P("ax", "circ", None, "rad"),
            P("ax", "circ", None, "rad"),
            P("ax", "circ", None, "rad"),
            P("ax", "circ", "rad", None, None, None),
            P("ax", "circ", "rad", None),
            P("ax", "circ"),
        ),
        out_specs=(P("ax", "circ", None, "rad"), P("ax", "circ", None, "rad")),
        check_vma=False,
    )
```

```python
import functools

import jax
import jax.numpy as jnp
from jax import lax
from jax.experimental import pallas as pl
from jax.experimental.pallas import tpu as pltpu
from jax.sharding import PartitionSpec as P

MESH = pl.DeviceIdType.MESH
F32 = jnp.float32
BF16 = jnp.bfloat16
GROUPS = 2
NLEV = 4
LOW_AX, UP_AX, LOW_C, UP_C = range(4)
FIRST = (0, 3, 6, 7)
WIDTH = (3, 3, 1, 1)
SLOTS = 8


def kernel(
    n_ax,
    n_circ,
    rhs,
    pivot,
    diagonal,
    coupling,
    pattern,
    level,
    first_out,
    second_out,
    h_all,
    pivots,
    diagonals,
    weights,
    fields,
    sends,
    lands,
    forward,
    first_result,
    second_result,
    images,
    first_swap,
    second_swap,
    joined,
    totals,
    order,
    ranks,
    near,
    faces,
    send_sem,
    recv_sem,
    local_sem,
    rad_send,
    rad_recv,
):
    results = (first_result, second_result)
    swaps = (first_swap, second_swap)
    tiles = rhs.shape[0]
    half = rhs.shape[1] // 2
    rows = half // GROUPS
    cells = rhs.shape[2]
    columns = tiles // 2
    per_level = tiles // NLEV

    ax = lax.axis_index("ax")
    circ = lax.axis_index("circ")
    rad = lax.axis_index("rad")
    other = 1 - rad
    targets = (
        {"ax": ax - 1},
        {"ax": ax + 1},
        {"circ": lax.rem(circ + n_circ - 1, n_circ)},
        {"circ": lax.rem(circ + 1, n_circ)},
    )
    sibling = {"rad": other}

    def at_direction(d, body):
        if d == LOW_AX:
            pl.when(ax > 0)(body)
        elif d == UP_AX:
            pl.when(ax < n_ax - 1)(body)
        else:
            body()

    my_lanes = pl.ds(pl.multiple_of(rad * cells, cells), cells)
    other_lanes = pl.ds(pl.multiple_of(other * cells, cells), cells)
    my_rows = pl.ds(pl.multiple_of(rad * half, half), half)
    other_rows = pl.ds(pl.multiple_of(other * half, half), half)

    for g in range(GROUPS):
        for c in range(2):
            lands[g, c] = jnp.zeros(lands.shape[2:], BF16)

    barrier = pltpu.get_barrier_semaphore()
    for d in (LOW_C, UP_C, LOW_AX, UP_AX):

        def greet(d=d):
            pl.semaphore_signal(barrier, inc=1, device_id=targets[d], device_id_type=MESH)

        at_direction(d, greet)
    pl.semaphore_signal(barrier, inc=1, device_id=sibling, device_id_type=MESH)

    local = [
        pltpu.make_async_copy(coupling, weights.at[rad], local_sem.at[0]),
        pltpu.make_async_copy(rhs.at[:, my_rows, :], h_all.at[:, :, my_lanes], local_sem.at[1]),
        pltpu.make_async_copy(pivot, pivots.at[:, :, my_lanes], local_sem.at[2]),
        pltpu.make_async_copy(diagonal, diagonals.at[:, :, my_lanes], local_sem.at[3]),
    ]
    for copy in local:
        copy.start()

    levels = [level[t] for t in range(tiles)]
    rank = []
    for t in range(tiles):
        before = jnp.int32(0)
        for u in range(tiles):
            if u < t:
                before = before + jnp.where(levels[u] <= levels[t], 1, 0)
            elif u > t:
                before = before + jnp.where(levels[u] < levels[t], 1, 0)
        rank.append(before)
        ranks[t] = before
    for j in range(tiles):
        found = jnp.int32(0)
        for t in range(tiles):
            found = found + jnp.where(rank[t] == j, t, 0)
        order[j] = found
    upper = 2 * per_level
    slot = [
        jnp.where(
            r >= upper,
            jnp.where(r >= upper + per_level, r - upper, r - per_level),
            jnp.where(r >= per_level, r - per_level, r),
        )
        for r in rank
    ]
    for t in range(tiles):
        row, column = t // columns, t % columns
        near[4 * t] = slot[t - columns] if row == 1 else jnp.int32(6 + column // 2)
        near[4 * t + 1] = slot[t + columns] if row == 0 else jnp.int32(9 + column // 2)
        near[4 * t + 2] = slot[t - 1] if column > 0 else jnp.int32(12)
        near[4 * t + 3] = slot[t + 1] if column < columns - 1 else jnp.int32(13)
    odd = lax.rem(levels[0], 2) == 1
    for c in range(2):
        for row in range(2):
            for j in range(3):
                even_column = slot[columns * row + 2 * j]
                odd_column = slot[columns * row + 2 * j + 1]
                if (c + row) % 2 == 0:
                    faces[SLOTS * c + 3 * row + j] = jnp.where(odd, odd_column, even_column)
                else:
                    faces[SLOTS * c + 3 * row + j] = jnp.where(odd, even_column, odd_column)
        low = (slot[0], slot[columns])
        high = (slot[columns - 1], slot[2 * columns - 1])
        faces[SLOTS * c + 6] = jnp.where(odd, low[1 - c], low[c])
        faces[SLOTS * c + 7] = jnp.where(odd, high[c], high[1 - c])

    local[0].wait()

    def keep_present(t, carry):
        for d in range(4):
            block = weights[rad, t, d * cells : (d + 1) * cells, :]
            weights[rad, t, d * cells : (d + 1) * cells, :] = jnp.where(
                pattern[t, d] != 0, block, jnp.zeros_like(block)
            )
        return carry

    lax.fori_loop(0, tiles, keep_present, 0)

    inner = (ax > 0) & (ax < n_ax - 1)
    pl.when(inner)(lambda: pl.semaphore_wait(barrier, 5))
    pl.when(jnp.logical_not(inner))(lambda: pl.semaphore_wait(barrier, 4))

    def to_sibling(index, source, target):
        return pltpu.make_async_remote_copy(
            src_ref=source,
            dst_ref=target,
            send_sem=rad_send.at[index],
            recv_sem=rad_recv.at[index],
            device_id=sibling,
            device_id_type=MESH,
        )

    shares = [
        to_sibling(0, rhs.at[:, other_rows, :], h_all.at[:, :, my_lanes]),
        to_sibling(1, pivot, pivots.at[:, :, my_lanes]),
        to_sibling(2, weights.at[rad], weights.at[rad]),
        to_sibling(3, diagonal, diagonals.at[:, :, my_lanes]),
    ]
    for share in shares:
        share.start()

    def exchange(g, c, d):
        opposite = d ^ 1
        return pltpu.make_async_remote_copy(
            src_ref=sends.at[g, c, pl.ds(FIRST[d], WIDTH[d])],
            dst_ref=lands.at[g, c, pl.ds(FIRST[opposite], WIDTH[d])],
            send_sem=send_sem.at[g, c, d],
            recv_sem=recv_sem.at[g, c, opposite],
            device_id=targets[d],
            device_id_type=MESH,
        )

    def arrival(g, c, d):
        return pltpu.make_async_remote_copy(
            src_ref=sends.at[g, c, pl.ds(FIRST[d], WIDTH[d])],
            dst_ref=lands.at[g, c, pl.ds(FIRST[d], WIDTH[d])],
            send_sem=send_sem.at[g, c, d],
            recv_sem=recv_sem.at[g, c, d],
            device_id=targets[d],
            device_id_type=MESH,
        )

    def sent(g, c):
        for d in range(4):
            at_direction(d, lambda d=d: exchange(g, c, d).wait_send())

    def send(g, c, again):
        if again:
            sent(g, c)
        for d in (LOW_C, UP_C, LOW_AX, UP_AX):
            for j in range(FIRST[d], FIRST[d] + WIDTH[d]):
                sends[g, c, j] = fields[g, c, faces[SLOTS * c + j]]
            at_direction(d, lambda d=d: exchange(g, c, d).start())

    def receive(g, c):
        for d in (LOW_AX, UP_AX, LOW_C, UP_C):
            at_direction(d, lambda d=d: arrival(g, c, d).wait_recv())
        fields[g, c, 6:] = lands[g, c]

    def neighbour_sum(g, c, k, t):
        for d in range(4):
            where = near[4 * t + d]
            for r in range(2):
                joined[k, r, :, d * cells : (d + 1) * cells] = fields[
                    g, c, where, :, r * cells : (r + 1) * cells
                ]
        for r in range(2):
            totals[k, :, r * cells : (r + 1) * cells] = jnp.dot(
                joined[k, r], weights[r, t], preferred_element_type=F32
            )
        return totals[k]

    def times(values, matrices, t):
        return jnp.dot(values, matrices[t], preferred_element_type=F32)

    zero = jnp.zeros((rows, 2 * cells), BF16)

    def groups(body):
        lax.fori_loop(0, GROUPS, lambda g, carry: (body(g), carry)[1], 0)

    def group_rows(g):
        return pl.ds(pl.multiple_of(g * rows, rows), rows)

    def local_slot(lev, k):
        return (lev // 2) * per_level + k

    def forward_level(application, lev, g):
        c = lev % 2
        if lev > 0:
            receive(g, 1 - c)
        for k in range(per_level):
            j = lev * per_level + k
            t = order[j]
            if application == 0:
                term = h_all[t, group_rows(g), :].astype(F32)
                if lev > 0:
                    term = term - neighbour_sum(g, 1 - c, k, t)
            else:
                term = images[g, j] + neighbour_sum(g, 1 - c, k, t)
            solved = times(term.astype(BF16), pivots, t).astype(BF16)
            forward[g, j] = solved
            if lev == NLEV - 1:
                results[application][g, j] = solved
                fields[g, c, local_slot(lev, k)] = solved
                fields[g, c, k] = zero
            elif application == 0:
                fields[g, c, local_slot(lev, k)] = solved
                if lev < 2:
                    fields[g, c, per_level + k] = zero
            else:
                rest_part = results[0][g, j].astype(F32) - solved.astype(F32)
                fields[g, c, local_slot(lev, k)] = rest_part.astype(BF16)

    def backward_level(application, lev, g):
        c = lev % 2
        receive(g, 1 - c)
        for k in range(per_level):
            j = lev * per_level + k
            t = order[j]
            total = neighbour_sum(g, 1 - c, k, t)
            value = forward[g, j].astype(F32) - times(total.astype(BF16), pivots, t)
            value = value.astype(BF16)
            results[application][g, j] = value
            if lev > 0:
                fields[g, c, local_slot(lev, k)] = value
                if lev == 2:
                    fields[g, c, k] = zero
            elif application == 0:
                image = (times(value, diagonals, t) + total).astype(BF16)
                solved = times(image, pivots, t).astype(BF16)
                forward[g, j] = solved
                rest_part = value.astype(F32) - solved.astype(F32)
                fields[g, c, k] = rest_part.astype(BF16)

    def image_part(lev, g):
        for k in range(per_level):
            j = lev * per_level + k
            images[g, j] = times(results[0][g, j], diagonals, order[j])

    def swap(application, g):
        mine = results[application]
        out = (first_out, second_out)[application]
        for t in range(tiles):
            out[t, pl.ds(pl.multiple_of(rad * half + g * rows, rows), rows), :] = mine[
                g, ranks[t], :, my_lanes
            ]
            swaps[application][t, group_rows(g), :] = mine[g, ranks[t], :, other_lanes]

    def hand_over(application):
        out = (first_out, second_out)[application]
        return to_sibling(4 + application, swaps[application], out.at[:, my_rows, :])

    def step(body, c, again=True):
        def run(g):
            body(g)
            if c is not None:
                send(g, c, again)

        groups(run)

    for index in (1, 2):
        local[index].wait()
    shares[0].wait_recv()
    shares[1].wait_recv()
    step(lambda g: forward_level(0, 0, g), 0, False)
    local[3].wait()
    shares[2].wait_recv()
    step(lambda g: forward_level(0, 1, g), 1, False)
    shares[3].wait_recv()
    step(lambda g: forward_level(0, 2, g), 0)
    step(lambda g: forward_level(0, 3, g), 1)
    step(lambda g: backward_level(0, 2, g), 0)
    groups(lambda g: (image_part(3, g), image_part(2, g)))
    step(lambda g: backward_level(0, 1, g), 1)
    groups(lambda g: image_part(1, g))
    step(lambda g: backward_level(0, 0, g), 0)
    groups(lambda g: swap(0, g))
    hand_over(0).start()
    step(lambda g: forward_level(1, 1, g), 1)
    step(lambda g: forward_level(1, 2, g), 0)
    step(lambda g: forward_level(1, 3, g), 1)
    step(lambda g: backward_level(1, 2, g), 0)
    step(lambda g: backward_level(1, 1, g), 1)
    step(lambda g: backward_level(1, 0, g), None)
    groups(lambda g: swap(1, g))
    hand_over(1).start()
    for g in range(GROUPS):
        for c in range(2):
            sent(g, c)
    for share in shares:
        share.wait_send()
    hand_over(0).wait()
    hand_over(1).wait()


def per_device(n_ax, n_circ, adjoint_rhs, pivot_inverse, diagonal_block, coupling, pattern, wave_level):
    tiles_axial, tiles_circ, rhs_count, cells = adjoint_rhs.shape
    tiles = tiles_axial * tiles_circ
    half = rhs_count // 2
    rows = half // GROUPS
    any_space = pl.BlockSpec(memory_space=pl.ANY)
    vmem = pl.BlockSpec(memory_space=pltpu.VMEM)
    smem = pl.BlockSpec(memory_space=pltpu.SMEM)
    tile = (rows, 2 * cells)
    out = jax.ShapeDtypeStruct((tiles, rhs_count, cells), BF16)
    first, second = pl.pallas_call(
        functools.partial(kernel, n_ax, n_circ),
        out_shape=(out, out),
        in_specs=[any_space] * 4 + [smem] * 2,
        out_specs=(vmem, vmem),
        scratch_shapes=[
            pltpu.VMEM((tiles, half, 2 * cells), BF16),
            pltpu.VMEM((tiles, 2 * cells, 2 * cells), BF16),
            pltpu.VMEM((tiles, 2 * cells, 2 * cells), BF16),
            pltpu.VMEM((2, tiles, 4 * cells, cells), BF16),
            pltpu.VMEM((GROUPS, 2, 6 + SLOTS, *tile), BF16),
            pltpu.VMEM((GROUPS, 2, SLOTS, *tile), BF16),
            pltpu.VMEM((GROUPS, 2, SLOTS, *tile), BF16),
            pltpu.VMEM((GROUPS, tiles, *tile), BF16),
            pltpu.VMEM((GROUPS, tiles, *tile), BF16),
            pltpu.VMEM((GROUPS, tiles, *tile), BF16),
            pltpu.VMEM((GROUPS, tiles, *tile), F32),
            pltpu.VMEM((tiles, half, cells), BF16),
            pltpu.VMEM((tiles, half, cells), BF16),
            pltpu.VMEM((tiles // NLEV, 2, rows, 4 * cells), BF16),
            pltpu.VMEM((tiles // NLEV, rows, 2 * cells), F32),
            pltpu.SMEM((tiles,), jnp.int32),
            pltpu.SMEM((tiles,), jnp.int32),
            pltpu.SMEM((4 * tiles,), jnp.int32),
            pltpu.SMEM((2 * SLOTS,), jnp.int32),
            pltpu.SemaphoreType.DMA((GROUPS, 2, 4)),
            pltpu.SemaphoreType.DMA((GROUPS, 2, 4)),
            pltpu.SemaphoreType.DMA((4,)),
            pltpu.SemaphoreType.DMA((6,)),
            pltpu.SemaphoreType.DMA((6,)),
        ],
        compiler_params=pltpu.CompilerParams(
            collective_id=0, has_side_effects=True, vmem_limit_bytes=40 << 20
        ),
    )(
        adjoint_rhs.reshape(tiles, rhs_count, cells),
        pivot_inverse.reshape(tiles, 2 * cells, cells),
        diagonal_block.reshape(tiles, 2 * cells, cells),
        coupling.reshape(tiles, 4 * cells, cells),
        pattern.reshape(tiles, 4),
        wave_level.reshape(tiles),
    )
    shape = (tiles_axial, tiles_circ, rhs_count, cells)
    return first.reshape(shape), second.reshape(shape)


def solution(mesh):
    return jax.shard_map(
        functools.partial(per_device, mesh.shape["ax"], mesh.shape["circ"]),
        mesh=mesh,
        in_specs=(
            P("ax", "circ", None, "rad"),
            P("ax", "circ", None, "rad"),
            P("ax", "circ", None, "rad"),
            P("ax", "circ", "rad", None, None, None),
            P("ax", "circ", "rad", None),
            P("ax", "circ"),
        ),
        out_specs=(P("ax", "circ", None, "rad"), P("ax", "circ", None, "rad")),
        check_vma=False,
    )
```

```python
import functools

import jax
import jax.numpy as jnp
from jax import lax
from jax.experimental import pallas as pl
from jax.experimental.pallas import tpu as pltpu
from jax.sharding import PartitionSpec as P

MESH = pl.DeviceIdType.MESH
F32 = jnp.float32
BF16 = jnp.bfloat16
GROUPS = 4
NLEV = 4
PARTS = 2
LOW_AX, UP_AX, LOW_C, UP_C = range(4)
FIRST = (0, 3, 6, 7)
WIDTH = (3, 3, 1, 1)
SLOTS = 8


def kernel(
    n_ax,
    n_circ,
    rhs,
    pivot,
    diagonal,
    coupling,
    pattern,
    level,
    first_out,
    second_out,
    h_all,
    pivots,
    diagonals,
    weights,
    own_weights,
    fields,
    sends,
    lands,
    forward,
    first_result,
    second_result,
    images,
    first_swap,
    second_swap,
    first_kept,
    second_kept,
    joined,
    totals,
    order,
    ranks,
    near,
    faces,
    send_sem,
    recv_sem,
    local_sem,
    rad_send,
    rad_recv,
):
    results = (first_result, second_result)
    swaps = (first_swap, second_swap)
    kept = (first_kept, second_kept)
    tiles = rhs.shape[0]
    half = rhs.shape[1] // 2
    rows = half // GROUPS
    cells = rhs.shape[2]
    columns = tiles // 2
    per_level = tiles // NLEV

    ax = lax.axis_index("ax")
    circ = lax.axis_index("circ")
    rad = lax.axis_index("rad")
    other = 1 - rad
    targets = (
        {"ax": ax - 1},
        {"ax": ax + 1},
        {"circ": lax.rem(circ + n_circ - 1, n_circ)},
        {"circ": lax.rem(circ + 1, n_circ)},
    )
    sibling = {"rad": other}

    def at_direction(d, body):
        if d == LOW_AX:
            pl.when(ax > 0)(body)
        elif d == UP_AX:
            pl.when(ax < n_ax - 1)(body)
        else:
            body()

    my_lanes = pl.ds(pl.multiple_of(rad * cells, cells), cells)
    other_lanes = pl.ds(pl.multiple_of(other * cells, cells), cells)
    my_rows = pl.ds(pl.multiple_of(rad * half, half), half)
    other_rows = pl.ds(pl.multiple_of(other * half, half), half)

    for g in range(GROUPS):
        for c in range(2):
            lands[g, c] = jnp.zeros(lands.shape[2:], BF16)

    barrier = pltpu.get_barrier_semaphore()
    for d in (LOW_C, UP_C, LOW_AX, UP_AX):

        def greet(d=d):
            pl.semaphore_signal(barrier, inc=1, device_id=targets[d], device_id_type=MESH)

        at_direction(d, greet)
    pl.semaphore_signal(barrier, inc=1, device_id=sibling, device_id_type=MESH)

    local = [
        pltpu.make_async_copy(coupling, own_weights, local_sem.at[0]),
        pltpu.make_async_copy(rhs.at[:, my_rows, :], h_all.at[:, :, my_lanes], local_sem.at[1]),
        pltpu.make_async_copy(pivot, pivots.at[:, :, my_lanes], local_sem.at[2]),
        pltpu.make_async_copy(diagonal, diagonals.at[:, :, my_lanes], local_sem.at[3]),
    ]
    for copy in local:
        copy.start()

    levels = [level[t // columns, t % columns] for t in range(tiles)]
    rank = []
    for t in range(tiles):
        before = jnp.int32(0)
        for u in range(tiles):
            if u < t:
                before = before + jnp.where(levels[u] <= levels[t], 1, 0)
            elif u > t:
                before = before + jnp.where(levels[u] < levels[t], 1, 0)
        rank.append(before)
        ranks[t] = before
    for j in range(tiles):
        found = jnp.int32(0)
        for t in range(tiles):
            found = found + jnp.where(rank[t] == j, t, 0)
        order[j] = found
    upper = 2 * per_level
    slot = [
        jnp.where(
            r >= upper,
            jnp.where(r >= upper + per_level, r - upper, r - per_level),
            jnp.where(r >= per_level, r - per_level, r),
        )
        for r in rank
    ]
    for t in range(tiles):
        row, column = t // columns, t % columns
        near[4 * t] = slot[t - columns] if row == 1 else jnp.int32(6 + column // 2)
        near[4 * t + 1] = slot[t + columns] if row == 0 else jnp.int32(9 + column // 2)
        near[4 * t + 2] = slot[t - 1] if column > 0 else jnp.int32(12)
        near[4 * t + 3] = slot[t + 1] if column < columns - 1 else jnp.int32(13)
    odd = lax.rem(levels[0], 2) == 1
    for c in range(2):
        for row in range(2):
            for j in range(3):
                even_column = slot[columns * row + 2 * j]
                odd_column = slot[columns * row + 2 * j + 1]
                if (c + row) % 2 == 0:
                    faces[SLOTS * c + 3 * row + j] = jnp.where(odd, odd_column, even_column)
                else:
                    faces[SLOTS * c + 3 * row + j] = jnp.where(odd, even_column, odd_column)
        low = (slot[0], slot[columns])
        high = (slot[columns - 1], slot[2 * columns - 1])
        faces[SLOTS * c + 6] = jnp.where(odd, low[1 - c], low[c])
        faces[SLOTS * c + 7] = jnp.where(odd, high[c], high[1 - c])

    local[0].wait()

    def keep_present(t, carry):
        for d in range(4):
            block = own_weights[t, d * cells : (d + 1) * cells, :]
            own_weights[t, d * cells : (d + 1) * cells, :] = jnp.where(
                pattern[t // columns, 0, d, lax.rem(t, columns)] != 0, block, jnp.zeros_like(block)
            )
        return carry

    lax.fori_loop(0, tiles, keep_present, 0)
    local.append(pltpu.make_async_copy(own_weights, weights.at[:, :, my_lanes], local_sem.at[4]))
    local[4].start()

    inner = (ax > 0) & (ax < n_ax - 1)
    pl.when(inner)(lambda: pl.semaphore_wait(barrier, 5))
    pl.when(jnp.logical_not(inner))(lambda: pl.semaphore_wait(barrier, 4))

    def to_sibling(index, source, target):
        return pltpu.make_async_remote_copy(
            src_ref=source,
            dst_ref=target,
            send_sem=rad_send.at[index],
            recv_sem=rad_recv.at[index],
            device_id=sibling,
            device_id_type=MESH,
        )

    shares = [
        to_sibling(0, rhs.at[:, other_rows, :], h_all.at[:, :, my_lanes]),
        to_sibling(1, pivot, pivots.at[:, :, my_lanes]),
        to_sibling(2, own_weights, weights.at[:, :, my_lanes]),
        to_sibling(3, diagonal, diagonals.at[:, :, my_lanes]),
    ]
    for share in shares:
        share.start()

    def exchange(g, c, d):
        opposite = d ^ 1
        return pltpu.make_async_remote_copy(
            src_ref=sends.at[g, c, pl.ds(FIRST[d], WIDTH[d])],
            dst_ref=lands.at[g, c, pl.ds(FIRST[opposite], WIDTH[d])],
            send_sem=send_sem.at[g, c, d],
            recv_sem=recv_sem.at[g, c, opposite],
            device_id=targets[d],
            device_id_type=MESH,
        )

    def arrival(g, c, d):
        return pltpu.make_async_remote_copy(
            src_ref=sends.at[g, c, pl.ds(FIRST[d], WIDTH[d])],
            dst_ref=lands.at[g, c, pl.ds(FIRST[d], WIDTH[d])],
            send_sem=send_sem.at[g, c, d],
            recv_sem=recv_sem.at[g, c, d],
            device_id=targets[d],
            device_id_type=MESH,
        )

    def sent(g, c):
        for d in range(4):
            at_direction(d, lambda d=d: exchange(g, c, d).wait_send())

    def send(g, c, again):
        if again:
            sent(g, c)
        for d in (LOW_C, UP_C, LOW_AX, UP_AX):
            for j in range(FIRST[d], FIRST[d] + WIDTH[d]):
                sends[g, c, j] = fields[g, c, faces[SLOTS * c + j]]
            at_direction(d, lambda d=d: exchange(g, c, d).start())

    def receive(g, c):
        for d in (LOW_AX, UP_AX, LOW_C, UP_C):
            at_direction(d, lambda d=d: arrival(g, c, d).wait_recv())
        fields[g, c, 6:] = lands[g, c]

    def neighbour_sum(g, c, k, t):
        for d in range(4):
            where = near[4 * t + d]
            for r in range(2):
                joined[k, r * rows : (r + 1) * rows, d * cells : (d + 1) * cells] = fields[
                    g, c, where, :, r * cells : (r + 1) * cells
                ]
        both = jnp.dot(joined[k], weights[t], preferred_element_type=F32)
        for r in range(2):
            totals[k, :, r * cells : (r + 1) * cells] = both[
                r * rows : (r + 1) * rows, r * cells : (r + 1) * cells
            ]
        return totals[k]

    def times(values, matrices, t):
        return jnp.dot(values, matrices[t], preferred_element_type=F32)

    zero = jnp.zeros((rows, 2 * cells), BF16)

    def groups(body):
        lax.fori_loop(0, GROUPS, lambda g, carry: (body(g), carry)[1], 0)

    def group_rows(g):
        return pl.ds(pl.multiple_of(g * rows, rows), rows)

    def local_slot(lev, k):
        return (lev // 2) * per_level + k

    def forward_level(application, lev, g):
        c = lev % 2
        if lev > 0:
            receive(g, 1 - c)
        for k in range(per_level):
            j = lev * per_level + k
            t = order[j]
            if application == 0:
                term = h_all[t, group_rows(g), :].astype(F32)
                if lev > 0:
                    term = term - neighbour_sum(g, 1 - c, k, t)
            else:
                term = images[g, j] + neighbour_sum(g, 1 - c, k, t)
            solved = times(term.astype(BF16), pivots, t).astype(BF16)
            forward[g, j] = solved
            if lev == NLEV - 1:
                results[application][g, j] = solved
                fields[g, c, local_slot(lev, k)] = solved
                fields[g, c, k] = zero
            elif application == 0:
                fields[g, c, local_slot(lev, k)] = solved
                if lev < 2:
                    fields[g, c, per_level + k] = zero
            else:
                rest_part = results[0][g, j].astype(F32) - solved.astype(F32)
                fields[g, c, local_slot(lev, k)] = rest_part.astype(BF16)

    def backward_level(application, lev, g):
        c = lev % 2
        receive(g, 1 - c)
        for k in range(per_level):
            j = lev * per_level + k
            t = order[j]
            total = neighbour_sum(g, 1 - c, k, t)
            value = forward[g, j].astype(F32) - times(total.astype(BF16), pivots, t)
            value = value.astype(BF16)
            results[application][g, j] = value
            if lev > 0:
                fields[g, c, local_slot(lev, k)] = value
                if lev == 2:
                    fields[g, c, k] = zero
            elif application == 0:
                image = (times(value, diagonals, t) + total).astype(BF16)
                solved = times(image, pivots, t).astype(BF16)
                forward[g, j] = solved
                rest_part = value.astype(F32) - solved.astype(F32)
                fields[g, c, k] = rest_part.astype(BF16)

    def image_part(lev, g):
        for k in range(per_level):
            j = lev * per_level + k
            images[g, j] = times(results[0][g, j], diagonals, order[j])

    def swap(application, g):
        mine = results[application]
        for t in range(tiles):
            kept[application][t, group_rows(g), :] = mine[g, ranks[t], :, my_lanes]
            swaps[application][t, group_rows(g), :] = mine[g, ranks[t], :, other_lanes]

    def hand_over(g):
        group_of_all = pl.ds(pl.multiple_of(rad * half + g * rows, rows), rows)
        return (
            to_sibling(
                5 + g, second_swap.at[:, group_rows(g), :], second_out.at[:, group_of_all, :]
            ),
            pltpu.make_async_copy(
                second_kept.at[:, group_rows(g), :],
                second_out.at[:, group_of_all, :],
                local_sem.at[6 + g],
            ),
        )

    first_hand_over = (
        to_sibling(4, first_swap, first_out.at[:, my_rows, :]),
        pltpu.make_async_copy(first_kept, first_out.at[:, my_rows, :], local_sem.at[5]),
    )

    def step(body, c, again=True):
        def run(g):
            body(g)
            if c is not None:
                send(g, c, again)

        groups(run)

    for index in (1, 2):
        local[index].wait()
    shares[0].wait_recv()
    shares[1].wait_recv()
    step(lambda g: forward_level(0, 0, g), 0, False)
    local[3].wait()
    local[4].wait()
    shares[2].wait_recv()
    step(lambda g: forward_level(0, 1, g), 1, False)
    shares[3].wait_recv()
    step(lambda g: forward_level(0, 2, g), 0)
    step(lambda g: forward_level(0, 3, g), 1)
    step(lambda g: backward_level(0, 2, g), 0)
    groups(lambda g: (image_part(3, g), image_part(2, g)))
    step(lambda g: backward_level(0, 1, g), 1)
    groups(lambda g: image_part(1, g))
    step(lambda g: backward_level(0, 0, g), 0)
    groups(lambda g: swap(0, g))
    for copy in first_hand_over:
        copy.start()
    step(lambda g: forward_level(1, 1, g), 1)
    step(lambda g: forward_level(1, 2, g), 0)
    step(lambda g: forward_level(1, 3, g), 1)
    step(lambda g: backward_level(1, 2, g), 0)
    step(lambda g: backward_level(1, 1, g), 1)

    def finish(g):
        backward_level(1, 0, g)
        swap(1, g)
        for copy in hand_over(g):
            copy.start()

    groups(finish)
    for g in range(GROUPS):
        for c in range(2):
            sent(g, c)
    for share in shares:
        share.wait_send()
    for copy in first_hand_over:
        copy.wait()
    for g in range(GROUPS):
        for copy in hand_over(g):
            copy.wait()


def write_out(first, second, first_out, second_out):
    first_out[...] = first[...]
    second_out[...] = second[...]


def per_device(n_ax, n_circ, adjoint_rhs, pivot_inverse, diagonal_block, coupling, pattern, wave_level):
    tiles_axial, tiles_circ, rhs_count, cells = adjoint_rhs.shape
    tiles = tiles_axial * tiles_circ
    half = rhs_count // 2
    rows = half // GROUPS
    hbm = pl.BlockSpec(memory_space=pl.ANY)
    smem = pl.BlockSpec(memory_space=pltpu.SMEM)
    tile = (rows, 2 * cells)
    out = jax.ShapeDtypeStruct((tiles, rhs_count, cells), BF16)
    first, second = pl.pallas_call(
        functools.partial(kernel, n_ax, n_circ),
        out_shape=(out, out),
        in_specs=[hbm] * 4 + [smem] * 2,
        out_specs=(hbm, hbm),
        scratch_shapes=[
            pltpu.VMEM((tiles, half, 2 * cells), BF16),
            pltpu.VMEM((tiles, 2 * cells, 2 * cells), BF16),
            pltpu.VMEM((tiles, 2 * cells, 2 * cells), BF16),
            pltpu.VMEM((tiles, 4 * cells, 2 * cells), BF16),
            pltpu.VMEM((tiles, 4 * cells, cells), BF16),
            pltpu.VMEM((GROUPS, 2, 6 + SLOTS, *tile), BF16),
            pltpu.VMEM((GROUPS, 2, SLOTS, *tile), BF16),
            pltpu.VMEM((GROUPS, 2, SLOTS, *tile), BF16),
            pltpu.VMEM((GROUPS, tiles, *tile), BF16),
            pltpu.VMEM((GROUPS, tiles, *tile), BF16),
            pltpu.VMEM((GROUPS, tiles, *tile), BF16),
            pltpu.VMEM((GROUPS, tiles, *tile), F32),
            pltpu.VMEM((tiles, half, cells), BF16),
            pltpu.VMEM((tiles, half, cells), BF16),
            pltpu.VMEM((tiles, half, cells), BF16),
            pltpu.VMEM((tiles, half, cells), BF16),
            pltpu.VMEM((tiles // NLEV, 2 * rows, 4 * cells), BF16),
            pltpu.VMEM((tiles // NLEV, rows, 2 * cells), F32),
            pltpu.SMEM((tiles,), jnp.int32),
            pltpu.SMEM((tiles,), jnp.int32),
            pltpu.SMEM((4 * tiles,), jnp.int32),
            pltpu.SMEM((2 * SLOTS,), jnp.int32),
            pltpu.SemaphoreType.DMA((GROUPS, 2, 4)),
            pltpu.SemaphoreType.DMA((GROUPS, 2, 4)),
            pltpu.SemaphoreType.DMA((6 + GROUPS,)),
            pltpu.SemaphoreType.DMA((5 + GROUPS,)),
            pltpu.SemaphoreType.DMA((5 + GROUPS,)),
        ],
        compiler_params=pltpu.CompilerParams(
            collective_id=0, has_side_effects=True, vmem_limit_bytes=60 << 20
        ),
    )(
        adjoint_rhs.reshape(tiles, rhs_count, cells),
        pivot_inverse.reshape(tiles, 2 * cells, cells),
        diagonal_block.reshape(tiles, 2 * cells, cells),
        coupling.reshape(tiles, 4 * cells, cells),
        jnp.transpose(pattern, (0, 2, 3, 1)),
        wave_level,
    )
    part = pl.BlockSpec((tiles // PARTS, rhs_count, cells), lambda i: (i, 0, 0))
    first, second = pl.pallas_call(
        write_out,
        out_shape=(out, out),
        grid=(PARTS,),
        in_specs=[part] * 2,
        out_specs=(part, part),
    )(first, second)
    shape = (tiles_axial, tiles_circ, rhs_count, cells)
    return first.reshape(shape), second.reshape(shape)


def solution(mesh):
    return jax.shard_map(
        functools.partial(per_device, mesh.shape["ax"], mesh.shape["circ"]),
        mesh=mesh,
        in_specs=(
            P("ax", "circ", None, "rad"),
            P("ax", "circ", None, "rad"),
            P("ax", "circ", None, "rad"),
            P("ax", "circ", "rad", None, None, None),
            P("ax", "circ", "rad", None),
            P("ax", "circ"),
        ),
        out_specs=(P("ax", "circ", None, "rad"), P("ax", "circ", None, "rad")),
        check_vma=False,
    )
```

```python
import functools

import jax
import jax.numpy as jnp
from jax import lax
from jax.experimental import pallas as pl
from jax.experimental.pallas import tpu as pltpu
from jax.sharding import PartitionSpec as P

MESH = pl.DeviceIdType.MESH
F32 = jnp.float32
BF16 = jnp.bfloat16
GROUPS = 4
NLEV = 4
PARTS = 2
LOW_AX, UP_AX, LOW_C, UP_C = range(4)
FIRST = (0, 3, 6, 7)
WIDTH = (3, 3, 1, 1)
SLOTS = 8


def kernel(
    n_ax,
    n_circ,
    rhs,
    pivot,
    diagonal,
    coupling,
    pattern,
    level,
    first_out,
    second_out,
    h_all,
    pivots,
    diagonals,
    weights,
    own_weights,
    fields,
    sends,
    lands,
    forward,
    first_result,
    second_result,
    images,
    first_swap,
    second_swap,
    first_kept,
    second_kept,
    joined,
    totals,
    order,
    ranks,
    near,
    faces,
    send_sem,
    recv_sem,
    local_sem,
    rad_send,
    rad_recv,
):
    results = (first_result, second_result)
    swaps = (first_swap, second_swap)
    kept = (first_kept, second_kept)
    tiles = rhs.shape[0]
    half = rhs.shape[1] // 2
    rows = half // GROUPS
    cells = rhs.shape[2]
    columns = tiles // 2
    per_level = tiles // NLEV

    ax = lax.axis_index("ax")
    circ = lax.axis_index("circ")
    rad = lax.axis_index("rad")
    other = 1 - rad
    targets = (
        {"ax": ax - 1},
        {"ax": ax + 1},
        {"circ": lax.rem(circ + n_circ - 1, n_circ)},
        {"circ": lax.rem(circ + 1, n_circ)},
    )
    sibling = {"rad": other}

    def at_direction(d, body):
        if d == LOW_AX:
            pl.when(ax > 0)(body)
        elif d == UP_AX:
            pl.when(ax < n_ax - 1)(body)
        else:
            body()

    my_lanes = pl.ds(pl.multiple_of(rad * cells, cells), cells)
    other_lanes = pl.ds(pl.multiple_of(other * cells, cells), cells)
    my_rows = pl.ds(pl.multiple_of(rad * half, half), half)
    other_rows = pl.ds(pl.multiple_of(other * half, half), half)

    for g in range(GROUPS):
        for c in range(2):
            lands[g, c] = jnp.zeros(lands.shape[2:], BF16)

    barrier = pltpu.get_barrier_semaphore()
    for d in (LOW_C, UP_C, LOW_AX, UP_AX):

        def greet(d=d):
            pl.semaphore_signal(barrier, inc=1, device_id=targets[d], device_id_type=MESH)

        at_direction(d, greet)
    pl.semaphore_signal(barrier, inc=1, device_id=sibling, device_id_type=MESH)

    local = [
        pltpu.make_async_copy(coupling, own_weights, local_sem.at[0]),
        pltpu.make_async_copy(rhs.at[:, my_rows, :], h_all.at[:, :, my_lanes], local_sem.at[1]),
        pltpu.make_async_copy(pivot, pivots.at[:, :, my_lanes], local_sem.at[2]),
        pltpu.make_async_copy(diagonal, diagonals.at[:, :, my_lanes], local_sem.at[3]),
    ]
    for copy in local:
        copy.start()

    levels = [level[t // columns, t % columns] for t in range(tiles)]
    rank = []
    for t in range(tiles):
        before = jnp.int32(0)
        for u in range(tiles):
            if u < t:
                before = before + jnp.where(levels[u] <= levels[t], 1, 0)
            elif u > t:
                before = before + jnp.where(levels[u] < levels[t], 1, 0)
        rank.append(before)
        ranks[t] = before
    for j in range(tiles):
        found = jnp.int32(0)
        for t in range(tiles):
            found = found + jnp.where(rank[t] == j, t, 0)
        order[j] = found
    upper = 2 * per_level
    slot = [
        jnp.where(
            r >= upper,
            jnp.where(r >= upper + per_level, r - upper, r - per_level),
            jnp.where(r >= per_level, r - per_level, r),
        )
        for r in rank
    ]
    for t in range(tiles):
        row, column = t // columns, t % columns
        near[4 * t] = slot[t - columns] if row == 1 else jnp.int32(6 + column // 2)
        near[4 * t + 1] = slot[t + columns] if row == 0 else jnp.int32(9 + column // 2)
        near[4 * t + 2] = slot[t - 1] if column > 0 else jnp.int32(12)
        near[4 * t + 3] = slot[t + 1] if column < columns - 1 else jnp.int32(13)
    odd = lax.rem(levels[0], 2) == 1
    for c in range(2):
        for row in range(2):
            for j in range(3):
                even_column = slot[columns * row + 2 * j]
                odd_column = slot[columns * row + 2 * j + 1]
                if (c + row) % 2 == 0:
                    faces[SLOTS * c + 3 * row + j] = jnp.where(odd, odd_column, even_column)
                else:
                    faces[SLOTS * c + 3 * row + j] = jnp.where(odd, even_column, odd_column)
        low = (slot[0], slot[columns])
        high = (slot[columns - 1], slot[2 * columns - 1])
        faces[SLOTS * c + 6] = jnp.where(odd, low[1 - c], low[c])
        faces[SLOTS * c + 7] = jnp.where(odd, high[c], high[1 - c])

    local[0].wait()

    def keep_present(t, carry):
        for d in range(4):
            block = own_weights[t, d * cells : (d + 1) * cells, :]
            own_weights[t, d * cells : (d + 1) * cells, :] = jnp.where(
                pattern[t // columns, 0, d, lax.rem(t, columns)] != 0, block, jnp.zeros_like(block)
            )
        return carry

    lax.fori_loop(0, tiles, keep_present, 0)
    local.append(pltpu.make_async_copy(own_weights, weights.at[:, :, my_lanes], local_sem.at[4]))
    local[4].start()

    inner = (ax > 0) & (ax < n_ax - 1)
    pl.when(inner)(lambda: pl.semaphore_wait(barrier, 5))
    pl.when(jnp.logical_not(inner))(lambda: pl.semaphore_wait(barrier, 4))

    def to_sibling(index, source, target):
        return pltpu.make_async_remote_copy(
            src_ref=source,
            dst_ref=target,
            send_sem=rad_send.at[index],
            recv_sem=rad_recv.at[index],
            device_id=sibling,
            device_id_type=MESH,
        )

    shares = [
        to_sibling(0, rhs.at[:, other_rows, :], h_all.at[:, :, my_lanes]),
        to_sibling(1, pivot, pivots.at[:, :, my_lanes]),
        to_sibling(2, own_weights, weights.at[:, :, my_lanes]),
        to_sibling(3, diagonal, diagonals.at[:, :, my_lanes]),
    ]
    for share in shares:
        share.start()

    def exchange(g, c, d):
        opposite = d ^ 1
        return pltpu.make_async_remote_copy(
            src_ref=sends.at[g, c, pl.ds(FIRST[d], WIDTH[d])],
            dst_ref=lands.at[g, c, pl.ds(FIRST[opposite], WIDTH[d])],
            send_sem=send_sem.at[g, c, d],
            recv_sem=recv_sem.at[g, c, opposite],
            device_id=targets[d],
            device_id_type=MESH,
        )

    def arrival(g, c, d):
        return pltpu.make_async_remote_copy(
            src_ref=sends.at[g, c, pl.ds(FIRST[d], WIDTH[d])],
            dst_ref=lands.at[g, c, pl.ds(FIRST[d], WIDTH[d])],
            send_sem=send_sem.at[g, c, d],
            recv_sem=recv_sem.at[g, c, d],
            device_id=targets[d],
            device_id_type=MESH,
        )

    def sent(g, c):
        for d in range(4):
            at_direction(d, lambda d=d: exchange(g, c, d).wait_send())

    def send(g, c, again):
        if again:
            sent(g, c)
        for d in (LOW_C, UP_C, LOW_AX, UP_AX):
            for j in range(FIRST[d], FIRST[d] + WIDTH[d]):
                sends[g, c, j] = fields[g, c, faces[SLOTS * c + j]]
            at_direction(d, lambda d=d: exchange(g, c, d).start())

    def receive(g, c):
        for d in (LOW_AX, UP_AX, LOW_C, UP_C):
            at_direction(d, lambda d=d: arrival(g, c, d).wait_recv())
        fields[g, c, 6:] = lands[g, c]

    def neighbour_sums(g, c, chosen):
        beside = [[fields[g, c, near[4 * t + d]] for d in range(4)] for t in chosen]
        for k in range(per_level):
            for d in range(4):
                for r in range(2):
                    joined[k, r * rows : (r + 1) * rows, d * cells : (d + 1) * cells] = beside[k][
                        d
                    ][:, r * cells : (r + 1) * cells]
        both = [
            jnp.dot(joined[k], weights[t], preferred_element_type=F32)
            for k, t in enumerate(chosen)
        ]
        for k in range(per_level):
            for r in range(2):
                totals[k, :, r * cells : (r + 1) * cells] = both[k][
                    r * rows : (r + 1) * rows, r * cells : (r + 1) * cells
                ]
        return [totals[k] for k in range(per_level)]

    def times(values, matrices, t):
        return jnp.dot(values, matrices[t], preferred_element_type=F32)

    zero = jnp.zeros((rows, 2 * cells), BF16)

    def groups(body):
        lax.fori_loop(0, GROUPS, lambda g, carry: (body(g), carry)[1], 0)

    def group_rows(g):
        return pl.ds(pl.multiple_of(g * rows, rows), rows)

    def local_slot(lev, k):
        return (lev // 2) * per_level + k

    def forward_level(application, lev, g):
        c = lev % 2
        places = [lev * per_level + k for k in range(per_level)]
        chosen = [order[j] for j in places]
        if application == 0:
            terms = [h_all[t, group_rows(g), :].astype(F32) for t in chosen]
        else:
            terms = [images[g, j] for j in places]
        if lev > 0:
            receive(g, 1 - c)
            sums = neighbour_sums(g, 1 - c, chosen)
            if application == 0:
                terms = [term - total for term, total in zip(terms, sums)]
            else:
                terms = [term + total for term, total in zip(terms, sums)]
        solved = [
            times(term.astype(BF16), pivots, t).astype(BF16) for term, t in zip(terms, chosen)
        ]
        if application == 1 and lev < NLEV - 1:
            firsts = [results[0][g, j].astype(F32) for j in places]
        for k, j in enumerate(places):
            forward[g, j] = solved[k]
            if lev == NLEV - 1:
                results[application][g, j] = solved[k]
                fields[g, c, local_slot(lev, k)] = solved[k]
                fields[g, c, k] = zero
            elif application == 0:
                fields[g, c, local_slot(lev, k)] = solved[k]
                if lev < 2:
                    fields[g, c, per_level + k] = zero
            else:
                rest_part = firsts[k] - solved[k].astype(F32)
                fields[g, c, local_slot(lev, k)] = rest_part.astype(BF16)

    def backward_level(application, lev, g):
        c = lev % 2
        places = [lev * per_level + k for k in range(per_level)]
        chosen = [order[j] for j in places]
        forwards = [forward[g, j].astype(F32) for j in places]
        receive(g, 1 - c)
        sums = neighbour_sums(g, 1 - c, chosen)
        values = [
            (forwards[k] - times(sums[k].astype(BF16), pivots, t)).astype(BF16)
            for k, t in enumerate(chosen)
        ]
        if lev == 0 and application == 0:
            pictures = [
                (times(values[k], diagonals, t) + sums[k]).astype(BF16)
                for k, t in enumerate(chosen)
            ]
            solved = [times(pictures[k], pivots, t).astype(BF16) for k, t in enumerate(chosen)]
        for k, j in enumerate(places):
            results[application][g, j] = values[k]
            if lev > 0:
                fields[g, c, local_slot(lev, k)] = values[k]
                if lev == 2:
                    fields[g, c, k] = zero
            elif application == 0:
                forward[g, j] = solved[k]
                rest_part = values[k].astype(F32) - solved[k].astype(F32)
                fields[g, c, k] = rest_part.astype(BF16)

    def image_part(lev, g):
        for k in range(per_level):
            j = lev * per_level + k
            images[g, j] = times(results[0][g, j], diagonals, order[j])

    def swap(application, g):
        mine = results[application]
        for t in range(tiles):
            kept[application][t, group_rows(g), :] = mine[g, ranks[t], :, my_lanes]
            swaps[application][t, group_rows(g), :] = mine[g, ranks[t], :, other_lanes]

    def hand_over(g):
        group_of_all = pl.ds(pl.multiple_of(rad * half + g * rows, rows), rows)
        return (
            to_sibling(
                5 + g, second_swap.at[:, group_rows(g), :], second_out.at[:, group_of_all, :]
            ),
            pltpu.make_async_copy(
                second_kept.at[:, group_rows(g), :],
                second_out.at[:, group_of_all, :],
                local_sem.at[6 + g],
            ),
        )

    first_hand_over = (
        to_sibling(4, first_swap, first_out.at[:, my_rows, :]),
        pltpu.make_async_copy(first_kept, first_out.at[:, my_rows, :], local_sem.at[5]),
    )

    def step(body, c, again=True):
        def run(g):
            body(g)
            if c is not None:
                send(g, c, again)

        groups(run)

    for index in (1, 2):
        local[index].wait()
    shares[0].wait_recv()
    shares[1].wait_recv()
    step(lambda g: forward_level(0, 0, g), 0, False)
    local[3].wait()
    local[4].wait()
    shares[2].wait_recv()
    step(lambda g: forward_level(0, 1, g), 1, False)
    shares[3].wait_recv()
    step(lambda g: forward_level(0, 2, g), 0)
    step(lambda g: forward_level(0, 3, g), 1)
    step(lambda g: backward_level(0, 2, g), 0)
    groups(lambda g: (image_part(3, g), image_part(2, g)))
    step(lambda g: backward_level(0, 1, g), 1)
    groups(lambda g: image_part(1, g))
    step(lambda g: backward_level(0, 0, g), 0)
    groups(lambda g: swap(0, g))
    for copy in first_hand_over:
        copy.start()
    step(lambda g: forward_level(1, 1, g), 1)
    step(lambda g: forward_level(1, 2, g), 0)
    step(lambda g: forward_level(1, 3, g), 1)
    step(lambda g: backward_level(1, 2, g), 0)
    step(lambda g: backward_level(1, 1, g), 1)

    def finish(g):
        backward_level(1, 0, g)
        swap(1, g)
        for copy in hand_over(g):
            copy.start()

    groups(finish)
    for g in range(GROUPS):
        for c in range(2):
            sent(g, c)
    for share in shares:
        share.wait_send()
    for copy in first_hand_over:
        copy.wait()
    for g in range(GROUPS):
        for copy in hand_over(g):
            copy.wait()


def write_out(first, second, first_out, second_out):
    first_out[...] = first[...]
    second_out[...] = second[...]


def per_device(n_ax, n_circ, adjoint_rhs, pivot_inverse, diagonal_block, coupling, pattern, wave_level):
    tiles_axial, tiles_circ, rhs_count, cells = adjoint_rhs.shape
    tiles = tiles_axial * tiles_circ
    half = rhs_count // 2
    rows = half // GROUPS
    hbm = pl.BlockSpec(memory_space=pl.ANY)
    smem = pl.BlockSpec(memory_space=pltpu.SMEM)
    tile = (rows, 2 * cells)
    out = jax.ShapeDtypeStruct((tiles, rhs_count, cells), BF16)
    first, second = pl.pallas_call(
        functools.partial(kernel, n_ax, n_circ),
        out_shape=(out, out),
        in_specs=[hbm] * 4 + [smem] * 2,
        out_specs=(hbm, hbm),
        scratch_shapes=[
            pltpu.VMEM((tiles, half, 2 * cells), BF16),
            pltpu.VMEM((tiles, 2 * cells, 2 * cells), BF16),
            pltpu.VMEM((tiles, 2 * cells, 2 * cells), BF16),
            pltpu.VMEM((tiles, 4 * cells, 2 * cells), BF16),
            pltpu.VMEM((tiles, 4 * cells, cells), BF16),
            pltpu.VMEM((GROUPS, 2, 6 + SLOTS, *tile), BF16),
            pltpu.VMEM((GROUPS, 2, SLOTS, *tile), BF16),
            pltpu.VMEM((GROUPS, 2, SLOTS, *tile), BF16),
            pltpu.VMEM((GROUPS, tiles, *tile), BF16),
            pltpu.VMEM((GROUPS, tiles, *tile), BF16),
            pltpu.VMEM((GROUPS, tiles, *tile), BF16),
            pltpu.VMEM((GROUPS, tiles, *tile), F32),
            pltpu.VMEM((tiles, half, cells), BF16),
            pltpu.VMEM((tiles, half, cells), BF16),
            pltpu.VMEM((tiles, half, cells), BF16),
            pltpu.VMEM((tiles, half, cells), BF16),
            pltpu.VMEM((tiles // NLEV, 2 * rows, 4 * cells), BF16),
            pltpu.VMEM((tiles // NLEV, rows, 2 * cells), F32),
            pltpu.SMEM((tiles,), jnp.int32),
            pltpu.SMEM((tiles,), jnp.int32),
            pltpu.SMEM((4 * tiles,), jnp.int32),
            pltpu.SMEM((2 * SLOTS,), jnp.int32),
            pltpu.SemaphoreType.DMA((GROUPS, 2, 4)),
            pltpu.SemaphoreType.DMA((GROUPS, 2, 4)),
            pltpu.SemaphoreType.DMA((6 + GROUPS,)),
            pltpu.SemaphoreType.DMA((5 + GROUPS,)),
            pltpu.SemaphoreType.DMA((5 + GROUPS,)),
        ],
        compiler_params=pltpu.CompilerParams(
            collective_id=0, has_side_effects=True, vmem_limit_bytes=60 << 20
        ),
    )(
        adjoint_rhs.reshape(tiles, rhs_count, cells),
        pivot_inverse.reshape(tiles, 2 * cells, cells),
        diagonal_block.reshape(tiles, 2 * cells, cells),
        coupling.reshape(tiles, 4 * cells, cells),
        jnp.transpose(pattern, (0, 2, 3, 1)),
        wave_level,
    )
    part = pl.BlockSpec((tiles // PARTS, rhs_count, cells), lambda i: (i, 0, 0))
    first, second = pl.pallas_call(
        write_out,
        out_shape=(out, out),
        grid=(PARTS,),
        in_specs=[part] * 2,
        out_specs=(part, part),
    )(first, second)
    shape = (tiles_axial, tiles_circ, rhs_count, cells)
    return first.reshape(shape), second.reshape(shape)


def solution(mesh):
    return jax.shard_map(
        functools.partial(per_device, mesh.shape["ax"], mesh.shape["circ"]),
        mesh=mesh,
        in_specs=(
            P("ax", "circ", None, "rad"),
            P("ax", "circ", None, "rad"),
            P("ax", "circ", None, "rad"),
            P("ax", "circ", "rad", None, None, None),
            P("ax", "circ", "rad", None),
            P("ax", "circ"),
        ),
        out_specs=(P("ax", "circ", None, "rad"), P("ax", "circ", None, "rad")),
        check_vma=False,
    )
```
